512 devices in a mesh: tm: 8 (over z_lo), height: 64 (over z_hi, y, x, core).
Axes of the slice: x: 4, y: 4, z: 16 (z_hi: 2, z_lo: 8; z = z_hi * 8 + z_lo), core: 2. Of those that a mesh axis runs over, the one named last changes fastest.
Arguments:
- features: bfloat16 [16, 512, 32, 512], P('tm', 'height'), may hold values from -6 to 6
- clip_frames: int32 [4], replicated, may hold values from 1 to 7, 16 in all
- conv_mid: bfloat16 [3, 3, 3, 512, 512], replicated, may hold values from -0.0546875 to 0.0546875
- bias_mid: float32 [512], replicated, may hold values from -3 to 3
- conv_latent: bfloat16 [3, 3, 3, 512, 16], replicated, may hold values from -0.0546875 to 0.0546875
- bias_latent: float32 [16], replicated, may hold values from -4 to 4
- patch_weight: bfloat16 [64, 3072], replicated, may hold values from -0.75 to 0.75
- patch_bias: float32 [3072], replicated, may hold values from -3 to 3
Outputs:
- embedded: bfloat16 [65536, 3072], P(('tm', 'height'))
The draws below stay inside these ranges and needn't reach their ends.
Inputs may be any that keep to these rules, and one draw needn't show every extreme that they name: `clip_frames`: latent frames of each clip in packing order; they sum to 16, and the longest clip has exactly 7.
All inputs are finite; a program needn't handle non-finite values.
Results may differ from the reference program's by a relative error of at most 0.0075.
Values may be sent and summed in bfloat16 or wider, within the bound.
A program may use at most 128 MiB of HBM per device.

```python
import math
import jax
import jax.numpy as jnp
import numpy as np
from jax import lax

C = 512
LAT = 16
DM = 3072
MAXF = 7
HB = 8
W = 32
BANDS = 64
NT = 16
HEIGHT = 512
CLIPS = 4
TOKENS = 65536


def shard_levels(rng, extent, split, least, largest):
    gain = 1.0
    for position, parts in split:
        heights = jax.random.uniform(jax.random.fold_in(jax.random.fold_in(rng, 6), position), (parts,), jnp.float32, least / len(split), largest / len(split))
        gain = gain * jnp.repeat(jnp.exp(heights), extent[position] // parts).reshape((-1,) + (1,) * (len(extent) - 1 - position))
    return gain


def split_up(number_of, total, reach, slope):
    portions = [(1 << 20) // math.isqrt(grade ** slope) + 1 for grade in range(2, number_of + 1)]
    rest, given = total - reach - (number_of - 1), [1] * (number_of - 1)
    while rest > 0:
        free = [i for i in range(number_of - 1) if given[i] < reach]
        mass, remaining = sum([portions[i] for i in free]), rest
        for i in free:
            extra = min(reach - given[i], max(1, remaining * portions[i] // mass), rest)
            given[i] = given[i] + extra
            rest = rest - extra
    return np.array([reach] + given)


def uneven_parts(own_key, amount, total, bound, slope):
    if amount == 2:
        one = jax.random.randint(own_key, (), max(1, total - bound), min(bound, total - 1) + 1)
        return jnp.stack([one, total - one])
    lengths = jnp.asarray(split_up(amount, total, bound, slope), jnp.int32)
    pairs = (amount - 1) // 2
    donor, taker = lengths[1:1 + 2 * pairs:2], lengths[2:2 + 2 * pairs:2]
    slack = jnp.minimum(donor - 1, bound - taker)
    passed = jax.random.randint(jax.random.fold_in(own_key, 1), (pairs,), 0, 1 << 20) % (slack + 1)
    lengths = lengths.at[1:1 + 2 * pairs:2].set(donor - passed).at[2:2 + 2 * pairs:2].set(taker + passed)
    return lengths[jax.random.permutation(jax.random.fold_in(own_key, 2), amount)]


def noise(rng, shape, deviation, most, cuts=(), kind=jnp.bfloat16):
    result = jax.random.normal(rng, shape, jnp.float32) * deviation
    if len(cuts) > 0:
        result = shard_levels(rng, shape, cuts, -0.22, 0.18) * result
    return jnp.clip(result, min=-most, max=most).astype(kind)


def setup_inputs(seed: int = 0) -> dict:
    arg_keys = jax.random.split(jax.random.key(seed), 9)
    return {
        "features": noise(arg_keys[0], (NT, HEIGHT, W, C), 1.0, 6.0, ((0, 8), (1, 64))),
        "clip_frames": uneven_parts(arg_keys[1], CLIPS, NT, MAXF, 1).astype(jnp.int32),
        "conv_mid": noise(arg_keys[2], (3, 3, 3, C, C), (27 * C) ** -0.5, 0.0546875),
        "bias_mid": noise(arg_keys[3], (C,), 0.5, 3.0, (), jnp.float32),
        "conv_latent": noise(arg_keys[4], (3, 3, 3, C, LAT), (27 * C) ** -0.5, 0.0546875),
        "bias_latent": noise(arg_keys[5], (LAT,), 1.0, 4.0, (), jnp.float32),
        "patch_weight": noise(arg_keys[6], (4 * LAT, DM), (4 * LAT) ** -0.5, 0.75),
        "patch_bias": noise(arg_keys[7], (DM,), 0.5, 3.0, (), jnp.float32),
    }


latent_scale = 0.476986


def source_lags(clip_frames, first_frame, frame_total):
    clip_starts = jnp.cumsum(clip_frames, dtype=jnp.int32) - clip_frames
    frame_index = first_frame + jnp.arange(frame_total, dtype=jnp.int32)
    clip_begin = jnp.max(jnp.where(clip_starts[None, :] <= frame_index[:, None], clip_starts[None, :], 0), axis=1)
    back_steps = jnp.arange(3, dtype=jnp.int32)
    return jnp.minimum(back_steps[:, None], (frame_index - clip_begin)[None, :]).astype(jnp.int32)


def frame_columns(block):
    row_count = block.shape[-3] - 2
    col_count = block.shape[-2]
    pad_widths = [(0, 0)] * (block.ndim - 2) + [(1, 1), (0, 0)]
    padded = jnp.pad(block, pad_widths)
    pieces = [padded[..., row_shift:row_shift + row_count, col_shift:col_shift + col_count, :] for row_shift in range(3) for col_shift in range(3)]
    return jnp.concatenate(pieces, axis=-1)


def causal_conv(activated, weight, lags):
    activated = lax.optimization_barrier(activated)
    frame_total, row_total, col_count, channels = activated.shape
    window_rows = HB * BANDS
    window_count = row_total // window_rows
    outputs = weight.shape[-1]
    taps = weight.reshape(3, 9 * channels, outputs).astype(jnp.float32)
    windows = activated.reshape(frame_total, window_count, window_rows, col_count, channels)
    padded = jnp.pad(windows, ((0, 0), (0, 0), (1, 1), (0, 0), (0, 0)))

    def one_frame(frame_index):
        summed = jnp.zeros((window_count, window_rows, col_count, outputs), jnp.float32)
        for back_step in range(3):
            source_frame = frame_index - lags[back_step, frame_index]
            frame = lax.dynamic_slice_in_dim(padded, source_frame, 1, 0)[0]
            columns = frame_columns(frame).astype(jnp.float32)
            summed = summed + jnp.einsum("nrwk,ko->nrwo", columns, taps[back_step])
        return summed.reshape(row_total, col_count, outputs)

    return lax.map(one_frame, jnp.arange(frame_total, dtype=jnp.int32))


def reference(features, clip_frames, conv_mid, bias_mid, conv_latent, bias_latent, patch_weight, patch_bias):
    lags = source_lags(clip_frames, jnp.int32(0), NT)
    act_first = jax.nn.silu(features.astype(jnp.float32)).astype(jnp.bfloat16)
    mixed = causal_conv(act_first, conv_mid, lags)
    hidden = (features.astype(jnp.float32) + mixed + bias_mid).astype(jnp.bfloat16)
    hidden = lax.optimization_barrier(hidden)
    act_second = jax.nn.silu(hidden.astype(jnp.float32)).astype(jnp.bfloat16)
    latent = (causal_conv(act_second, conv_latent, lags) + bias_latent) * latent_scale
    grid = latent.reshape(NT, HEIGHT // 2, 2, W // 2, 2, LAT).transpose(0, 3, 1, 5, 2, 4)
    patches = grid.reshape(TOKENS, 4 * LAT).astype(jnp.bfloat16)
    return (jnp.dot(patches, patch_weight, preferred_element_type=jnp.float32) + patch_bias).astype(jnp.bfloat16)
```

```python
import functools

import jax
import jax.numpy as jnp
from jax import lax
from jax.experimental import pallas as pl
from jax.experimental.pallas import tpu as pltpu
from jax.sharding import PartitionSpec as P

latent_scale = 0.476986
MESH = pl.DeviceIdType.MESH
f32, bf16 = jnp.float32, jnp.bfloat16

PREV, EVEN, ODD, NEXT = range(4)
ROUTES = (
    (0, 0, 0, (0, 1, 2)),
    (1, 0, 1, (1, 2)),
    (1, 1, 0, (0, 1, 2)),
    (2, 0, 2, (2,)),
    (2, 1, 1, (1, 2)),
    (3, 1, 2, (2,)),
)


def device(s, zh, y, x, core):
    return (s, zh * 32 + y * 8 + x * 2 + core)


def kernel(
    x_hbm, clips_hbm, wm_hbm, bm_hbm, wl_hbm, bl_hbm, pw_hbm, pb_hbm, out_hbm,
    raw, act, shifted, wm, acc, late_raw, late, act2, wl, conv2, outgoing, incoming, patches, pw, pwp, out, bm, bl, pb, clips,
    sem_x, sem_w, sem_small, sem_out, send_main, recv_main, send_edge, recv_edge, send_patch, recv_patch, send_extra, recv_extra,
    know_plane, know_four, know_all,
):
    s, h = lax.axis_index("tm"), lax.axis_index("height")
    zh, y, x, core = h // 32, (h // 8) % 4, (h // 2) % 4, h % 2
    other = (h + 32) % 64
    z = zh * 8 + s

    def along_z(step):
        there = (z + step + 16) % 16
        return device(there % 8, there // 8, y, x, core)

    def above(step):
        band = (h + step + 64) % 64
        wrapped = (band + 32) % 64
        down = ((s + 7) % 8, jnp.where(s == 0, wrapped, band))
        up = ((s + 1) % 8, jnp.where(s == 7, wrapped, band))
        return (s, band), down, up

    has_top, has_bottom = h % 32 != 0, h % 32 != 31
    (_, down, up) = above(0)
    band_next = jnp.where(s == 7, other, h)
    band_prev = jnp.where(s == 0, other, h)

    load_x = pltpu.make_async_copy(x_hbm, raw.at[pl.ds(EVEN, 2), pl.ds(1, 8)], sem_x)
    load_x.start()
    load_w = [pltpu.make_async_copy(wm_hbm.at[k], wm.at[k], sem_w.at[k]) for k in range(3)]
    load_clips = pltpu.make_async_copy(clips_hbm, clips, sem_small.at[0])
    load_clips.start()
    load_w[0].start()

    line = [device(s, zh, y, (x + d) % 4, c) for d in (1, 2, 3) for c in (0, 1)] + [device(s, zh, y, x, 1 - core)]
    column = [device(s, zh, (y + d) % 4, x, core) for d in (1, 2, 3)]
    near_z = [along_z(d) for d in (-2, -1, 1, 2)]
    barrier = pltpu.get_barrier_semaphore()
    for there in line + column + near_z:
        pl.semaphore_signal(barrier, inc=1, device_id=there, device_id_type=MESH)

    @pl.when(has_top)
    def _():
        for there in above(-1):
            pl.semaphore_signal(barrier, inc=1, device_id=there, device_id_type=MESH)

    @pl.when(has_bottom)
    def _():
        for there in above(1):
            pl.semaphore_signal(barrier, inc=1, device_id=there, device_id_type=MESH)

    pl.semaphore_wait(barrier, 14 + 3 * has_top.astype(jnp.int32) + 3 * has_bottom.astype(jnp.int32))

    main = []
    for half in range(2):
        ch = pl.ds(half * 256, 256)
        for i, (frame, slot, there) in enumerate(((0, NEXT, down), (1, PREV, up))):
            main.append(
                pltpu.make_async_remote_copy(
                    x_hbm.at[frame, :, :, ch], raw.at[slot, pl.ds(1, 8), :, ch],
                    send_main.at[i, half], recv_main.at[i, half], device_id=there, device_id_type=MESH,
                )
            )

    def edge_copies(side, to_late):
        here, lower, upper = above(2 * side - 1)
        row, there_row = (0, 9) if side == 0 else (7, 0)
        copies = []
        for slot, frame, there in ((EVEN, 0, here), (ODD, 1, here), (NEXT, 0, lower), (PREV, 1, upper)):
            target = late_raw.at[slot] if to_late else raw.at[slot, there_row]
            copies.append(
                pltpu.make_async_remote_copy(
                    x_hbm.at[frame, row], target, send_edge.at[slot, side], recv_edge.at[slot, side],
                    device_id=there, device_id_type=MESH,
                )
            )
        return copies

    @pl.when(has_top)
    def _():
        for c in edge_copies(0, False):
            c.start()

    @pl.when(has_bottom)
    def _():
        for c in edge_copies(1, False):
            c.start()

    for c in main:
        c.start()
    for there in column + near_z:
        pl.semaphore_signal(know_plane, inc=1, device_id=there, device_id_type=MESH)
    load_w[1].start()
    load_w[2].start()
    small = [
        pltpu.make_async_copy(a, b, sem_small.at[1 + i])
        for i, (a, b) in enumerate(((bm_hbm, bm), (bl_hbm, bl), (pw_hbm, pw), (pb_hbm, pb)))
    ]
    for c in small:
        c.start()
    wl[...] = jnp.zeros_like(wl)
    tap_copies = [
        pltpu.make_async_copy(wl_hbm.at[k, i, j], wl.at[j, pl.ds(k * 128 + i * 16, 16)], sem_small.at[5 + k * 9 + i * 3 + j])
        for k in range(3) for i in range(3) for j in range(3)
    ]
    for c in tap_copies:
        c.start()

    shifted[:, 0:8] = jnp.zeros((10, 8, 256), f32)
    shifted[:, 40:48] = jnp.zeros((10, 8, 256), f32)
    late_raw_zero = jnp.zeros((32, 512), bf16)

    def silu(v):
        return v / (1.0 + jnp.exp(-v))

    def prepare(slot, half):
        ch = slice(half * 256, half * 256 + 256)
        v = silu(raw[slot, :, :, ch].astype(f32))
        act[slot, 1, :, :, ch] = v.astype(bf16)
        shifted[:, 8:40] = v
        act[slot, 0, :, :, ch] = shifted[:, 7:39].astype(bf16)
        act[slot, 2, :, :, ch] = shifted[:, 9:41].astype(bf16)

    def await_edges(slot, band):
        top, bottom = band % 32 != 0, band % 32 != 31
        for there, row, side in ((top, 0, 1), (bottom, 9, 0)):

            @pl.when(there)
            def _():
                pltpu.make_async_copy(late_raw.at[slot], raw.at[slot, row], recv_edge.at[slot, side]).wait()

            @pl.when(jnp.logical_not(there))
            def _():
                raw[slot, row] = late_raw_zero

    load_x.wait()
    for slot in (EVEN, ODD):
        await_edges(slot, h)
        for half in range(2):
            prepare(slot, half)

    load_clips.wait()
    one, two = clips[0], clips[0] + clips[1]
    three = two + clips[2]

    def age(frame):
        begin = jnp.where(three <= frame, three, jnp.where(two <= frame, two, jnp.where(one <= frame, one, 0)))
        return frame - begin

    ages = [age((2 * s + 1 + d) % 16) for d in range(4)]
    lags = [[jnp.minimum(k, a) for k in range(3)] for a in ages]
    source = [[ODD - lags[0][k] for k in range(3)], [NEXT - lags[1][k] for k in range(3)]]
    source[0][0], source[1][0] = ODD, NEXT

    acc[...] = jnp.zeros_like(acc)

    def add_taps(output, k, half):
        slot = source[output][k]
        ch = slice(half * 256, half * 256 + 256)
        lhs = jnp.concatenate(
            [act[slot, j, i : i + 8, :, ch].reshape(256, 256) for i in range(3) for j in range(3)], axis=1
        )
        rhs = wm[k, :, :, ch].reshape(9 * 256, 512)
        acc[output] += jnp.dot(lhs, rhs, preferred_element_type=f32)

    load_w[0].wait()
    add_taps(0, 0, 0)
    add_taps(0, 0, 1)
    load_w[1].wait()
    add_taps(0, 1, 0)
    pl.semaphore_wait(know_plane, 7)
    for d in (-4, -3, -2, -1, 1, 2, 3, 4):
        pl.semaphore_signal(know_four, inc=1, device_id=along_z(d), device_id_type=MESH)
    add_taps(0, 1, 1)
    load_w[2].wait()
    await_edges(NEXT, band_next)
    await_edges(PREV, band_prev)
    for half in range(2):
        main[2 * half].wait_recv()
        main[2 * half + 1].wait_recv()
        prepare(NEXT, half)
        prepare(PREV, half)
        add_taps(0, 2, half)
        add_taps(1, 0, half)
        if half == 1:
            pl.semaphore_wait(know_four, 8)
            for d in (-4, 4):
                pl.semaphore_signal(know_all, inc=1, device_id=along_z(d), device_id_type=MESH)
        add_taps(1, 1, half)
        add_taps(1, 2, half)
    pl.semaphore_wait(know_all, 2)

    @pl.when(h == 32)
    def _():
        for c in edge_copies(0, True):
            c.start()

    @pl.when(h == 31)
    def _():
        for c in edge_copies(1, True):
            c.start()

    def is_edge(band):
        return jnp.logical_or(band == 31, band == 32)

    late_slots = ((EVEN, is_edge(h)), (ODD, is_edge(h)), (NEXT, is_edge(band_next)), (PREV, is_edge(band_prev)))

    @pl.when(jnp.logical_or(is_edge(h), is_edge(other)))
    def _():
        at_bottom = h % 32 == 31
        for slot, is_late in late_slots:

            @pl.when(jnp.logical_and(is_late, at_bottom))
            def _():
                pltpu.make_async_copy(late_raw.at[slot], late_raw.at[slot], recv_edge.at[slot, 0]).wait()

            @pl.when(jnp.logical_and(is_late, jnp.logical_not(at_bottom)))
            def _():
                pltpu.make_async_copy(late_raw.at[slot], late_raw.at[slot], recv_edge.at[slot, 1]).wait()

            @pl.when(jnp.logical_not(is_late))
            def _():
                late_raw[slot] = late_raw_zero

        for half in range(2):
            ch = slice(half * 256, half * 256 + 256)
            v = silu(late_raw[:, :, ch].astype(f32))
            late[:, 1, :, ch] = v.astype(bf16)
            shifted[0:4, 8:40] = v
            late[:, 0, :, ch] = shifted[0:4, 7:39].astype(bf16)
            late[:, 2, :, ch] = shifted[0:4, 9:41].astype(bf16)
        row = jnp.where(at_bottom, 7, 0)
        tap = jnp.where(at_bottom, 2, 0)
        total = None
        for k in range(3):
            lhs = jnp.concatenate(
                [jnp.concatenate([late[source[o][k], j] for j in range(3)], axis=1) for o in range(2)], axis=0
            )
            part = jnp.dot(lhs, wm[k, tap].reshape(3 * 512, 512), preferred_element_type=f32)
            total = part if total is None else total + part
        acc[:, pl.ds(pl.multiple_of(row * 32, 32), 32)] += total.reshape(2, 32, 512)

    small[0].wait()
    for output, slot in ((0, ODD), (1, NEXT)):
        here = raw[slot, 1:9].reshape(256, 512).astype(f32)
        hidden = (here + acc[output] + bm[...]).astype(bf16).astype(f32)
        act2[output] = silu(hidden).astype(bf16)

    for c in tap_copies:
        c.wait()
    conv2[:, :, :, 0:8] = jnp.zeros((3, 3, 16, 8, 128), f32)
    conv2[:, :, :, 40:48] = jnp.zeros((3, 3, 16, 8, 128), f32)
    for j in range(3):
        product = lax.dot_general(
            act2[...].reshape(512, 512), wl[j], (((1,), (1,)), ((), ())), preferred_element_type=f32
        )
        for k in range(3):
            conv2[k, j, :, 8:40] = product[:, k * 128 : k * 128 + 128].reshape(16, 32, 128)
    lane = lax.broadcasted_iota(jnp.int32, (16, 128), 1)
    groups = [lane // 16 == n for n in range(8)]
    totals = [[[] for _ in range(3)] for _ in range(4)]
    for parity in range(2):
        for d in range(4):
            value = None
            for dest, output, lag, taps in ROUTES:
                if dest != d:
                    continue
                for k in taps:
                    keep = (lags[d][k] == lag).astype(f32)
                    summed = None
                    for j in range(3):
                        part = conv2[k, j, output * 8 : output * 8 + 8, pl.ds(7 + j + parity, 16, stride=2)]
                        summed = part if summed is None else summed + part
                    summed = summed * keep
                    value = summed if value is None else value + summed
            for r in range(8):
                for i in range(3):
                    place = r - i + 3
                    index, a = place // 2, place % 2
                    group = index // 3 * 4 + a * 2 + parity
                    turned = pltpu.roll(value[r], (group - i) * 16 % 128, 1)
                    totals[d][index % 3].append(jnp.where(groups[group], turned, 0.0))
    for d in range(4):
        for n in range(3):
            outgoing[d, n] = functools.reduce(lambda p, q: p + q, totals[d][n])

    small[2].wait()
    for d in range(4):
        frame = (2 * s + 1 + d) % 16
        band = h if d == 0 else band_next
        role = d // 2
        slot = band % 32
        side = band // 32

        def send(q, there_core, target, sems, mine):
            there = (frame // 2, (frame % 2) * 32 + 2 * q + there_core)
            src = outgoing.at[d, :, q]
            if not mine:
                pltpu.make_async_remote_copy(
                    src, target, sems[0], sems[1], device_id=there, device_id_type=MESH
                ).start()
                return
            is_self = jnp.logical_and(there[0] == s, there[1] == h)

            @pl.when(is_self)
            def _():
                pltpu.make_async_copy(src, target, sems[1]).start()

            @pl.when(jnp.logical_not(is_self))
            def _():
                pltpu.make_async_remote_copy(
                    src, target, sems[0], sems[1], device_id=there, device_id_type=MESH
                ).start()

        @pl.loop(0, 16)
        def _(q):
            send(q, side, incoming.at[role, :, slot], (send_patch.at[d], recv_patch.at[role]), d == 0)

        @pl.when(is_edge(band))
        def _():
            @pl.loop(0, 16)
            def _(q):
                send(q, 1 - side, incoming.at[role, :, 32], (send_extra.at[d], recv_extra.at[role]), d == 0)

    to = lax.broadcasted_iota(jnp.int32, (64, 64), 0)
    at = lax.broadcasted_iota(jnp.int32, (64, 64), 1)
    move = (at == (to % 16) * 4 + to // 16).astype(bf16)
    pwp[...] = jnp.dot(move, pw[...], preferred_element_type=f32).astype(bf16)
    small[1].wait()
    small[3].wait()

    for role in range(2):
        arrived = incoming.at[role, :, pl.ds(0, 32)]
        pltpu.make_async_copy(arrived, arrived, recv_patch.at[role]).wait()
        arrived = incoming.at[role, :, 32]
        pltpu.make_async_copy(arrived, arrived, recv_extra.at[role]).wait()
    total = incoming[0] + incoming[1]
    band_row = lax.broadcasted_iota(jnp.int32, (32, 64), 0)
    piece = [total[n % 3, 0:32, (n // 3) * 64 : (n // 3) * 64 + 64] for n in range(6)]
    extra = total[:, 32:33]
    before = jnp.where(core == 1, extra[2, :, 64:128], 0.0)
    after = jnp.where(core == 0, extra[0, :, 0:64], 0.0)
    piece[1] += jnp.where(band_row == 0, before, pltpu.roll(piece[5], 1, 0))
    piece[4] += jnp.where(band_row == 31, after, pltpu.roll(piece[0], 31, 0))
    for n in range(4):
        patches[pl.ds(n, 32, stride=4), 0:64] = piece[1 + n]
    bias = jnp.concatenate([bl[...]] * 4, axis=1)
    latent = ((patches[:, 0:64] + bias) * latent_scale).astype(bf16)
    out[...] = (jnp.dot(latent, pwp[...], preferred_element_type=f32) + pb[...]).astype(bf16)
    write = pltpu.make_async_copy(out, out_hbm, sem_out)
    write.start()

    for c in main:
        c.wait_send()
    for side, sends in ((0, h != 0), (1, h != 63)):

        @pl.when(sends)
        def _():
            for c in edge_copies(side, False):
                c.wait_send()

    for d in range(4):
        band = h if d == 0 else band_next
        if d == 0:
            own = jnp.logical_and(zh == 1, core == 1)
            own_extra = h == 32
        else:
            own = own_extra = None
        for sem, sent, one_less in ((send_patch.at[d], None, own), (send_extra.at[d], is_edge(band), own_extra)):
            whole, less = outgoing.at[d], outgoing.at[d, :, pl.ds(0, 15)]

            def finish(sem=sem, one_less=one_less, whole=whole, less=less):
                if one_less is None:
                    pltpu.make_async_copy(whole, whole, sem).wait()
                    return

                @pl.when(one_less)
                def _():
                    pltpu.make_async_copy(less, less, sem).wait()

                @pl.when(jnp.logical_not(one_less))
                def _():
                    pltpu.make_async_copy(whole, whole, sem).wait()

            if sent is None:
                finish()
            else:
                pl.when(sent)(finish)
    write.wait()


def per_device(features, clip_frames, conv_mid, bias_mid, conv_latent, bias_latent, patch_weight, patch_bias):
    dma, regular = pltpu.SemaphoreType.DMA, pltpu.SemaphoreType.REGULAR
    anywhere = pl.BlockSpec(memory_space=pl.ANY)
    return pl.pallas_call(
        kernel,
        out_shape=jax.ShapeDtypeStruct((128, 3072), bf16),
        in_specs=[anywhere] * 8,
        out_specs=anywhere,
        scratch_shapes=[
            pltpu.VMEM((4, 10, 32, 512), bf16),
            pltpu.VMEM((4, 3, 10, 32, 512), bf16),
            pltpu.VMEM((10, 48, 256), f32),
            pltpu.VMEM((3, 3, 3, 512, 512), bf16),
            pltpu.VMEM((2, 256, 512), f32),
            pltpu.VMEM((4, 32, 512), bf16),
            pltpu.VMEM((4, 3, 32, 512), bf16),
            pltpu.VMEM((2, 256, 512), bf16),
            pltpu.VMEM((3, 384, 512), bf16),
            pltpu.VMEM((3, 3, 16, 48, 128), f32),
            pltpu.VMEM((4, 3, 16, 128), f32),
            pltpu.VMEM((2, 3, 40, 128), f32),
            pltpu.VMEM((128, 128), f32),
            pltpu.VMEM((64, 3072), bf16),
            pltpu.VMEM((64, 3072), bf16),
            pltpu.VMEM((128, 3072), bf16),
            pltpu.VMEM((1, 512), f32),
            pltpu.VMEM((1, 16), f32),
            pltpu.VMEM((1, 3072), f32),
            pltpu.SMEM((4,), jnp.int32),
            dma, dma((3,)), dma((32,)), dma,
            dma((2, 2)), dma((2, 2)), dma((4, 2)), dma((4, 2)),
            dma((4,)), dma((2,)), dma((4,)), dma((2,)),
            regular, regular, regular,
        ],
        compiler_params=pltpu.CompilerParams(
            collective_id=0, has_side_effects=True, vmem_limit_bytes=58 * 2**20
        ),
    )(
        features, clip_frames, conv_mid, bias_mid.reshape(1, -1), jnp.swapaxes(conv_latent, 3, 4),
        bias_latent.reshape(1, -1), patch_weight, patch_bias.reshape(1, -1),
    )


def solution(mesh):
    return jax.shard_map(
        per_device,
        mesh=mesh,
        in_specs=(P("tm", "height", None, None), P(), P(), P(), P(), P(), P(), P()),
        out_specs=P(("tm", "height"), None),
        check_vma=False,
    )
```

```python
import functools

import jax
import jax.numpy as jnp
from jax import lax
from jax.experimental import pallas as pl
from jax.experimental.pallas import tpu as pltpu
from jax.sharding import PartitionSpec as P

latent_scale = 0.476986
MESH = pl.DeviceIdType.MESH
f32, bf16 = jnp.float32, jnp.bfloat16

PREV, EVEN, ODD, NEXT = range(4)
ROUTES = (
    (0, 0, 0, (0, 1, 2)),
    (1, 0, 1, (1, 2)),
    (1, 1, 0, (0, 1, 2)),
    (2, 0, 2, (2,)),
    (2, 1, 1, (1, 2)),
    (3, 1, 2, (2,)),
)


def device(s, zh, y, x, core):
    return (s, zh * 32 + y * 8 + x * 2 + core)


def kernel(
    x_hbm, clips_hbm, wm_hbm, bm_hbm, wl_hbm, bl_hbm, out_hbm,
    raw, act, shifted, wm, acc, late_raw, late, act2, taps, wl, conv2, outgoing, incoming, patches, out, bm, bl, clips,
    sem_x, sem_w, sem_small, sem_out, send_main, recv_main, send_edge, recv_edge, send_patch, recv_patch, send_extra, recv_extra,
    know_plane, know_four, know_all, know_column, know_corners,
):
    s, h = lax.axis_index("tm"), lax.axis_index("height")
    zh, y, x, core = h // 32, (h // 8) % 4, (h // 2) % 4, h % 2
    other = (h + 32) % 64
    z = zh * 8 + s

    def along_z(step):
        there = (z + step + 16) % 16
        return device(there % 8, there // 8, y, x, core)

    def above(step):
        band = (h + step + 64) % 64
        wrapped = (band + 32) % 64
        down = ((s + 7) % 8, jnp.where(s == 0, wrapped, band))
        up = ((s + 1) % 8, jnp.where(s == 7, wrapped, band))
        return (s, band), down, up

    has_top, has_bottom = h % 32 != 0, h % 32 != 31
    (_, down, up) = above(0)
    band_next = jnp.where(s == 7, other, h)
    band_prev = jnp.where(s == 0, other, h)

    load_x = pltpu.make_async_copy(x_hbm, raw.at[pl.ds(EVEN, 2), pl.ds(1, 8)], sem_x)
    load_x.start()
    load_w = [pltpu.make_async_copy(wm_hbm.at[k, i], wm.at[k, i], sem_w.at[3 * k + i]) for k in range(3) for i in range(3)]
    load_clips = pltpu.make_async_copy(clips_hbm, clips, sem_small.at[0])
    load_clips.start()
    for c in load_w[:3]:
        c.start()

    line = [device(s, zh, y, (x + d) % 4, c) for d in (1, 2, 3) for c in (0, 1)] + [device(s, zh, y, x, 1 - core)]
    column = [device(s, zh, (y + d) % 4, x, core) for d in (1, 2, 3)]
    near_z = [along_z(d) for d in (-2, -1, 1, 2)]
    barrier = pltpu.get_barrier_semaphore()
    for there in line + column + near_z:
        pl.semaphore_signal(barrier, inc=1, device_id=there, device_id_type=MESH)

    @pl.when(has_top)
    def _():
        pl.semaphore_signal(barrier, inc=1, device_id=above(-1)[0], device_id_type=MESH)

    @pl.when(has_bottom)
    def _():
        pl.semaphore_signal(barrier, inc=1, device_id=above(1)[0], device_id_type=MESH)

    at_corner = jnp.logical_or(h % 32 == 0, h % 32 == 31)
    opposite = (s, zh * 32 + 31 - h % 32)
    corner_z = [along_z(d) for d in (-4, -3, 3, 4)]

    @pl.when(at_corner)
    def _():
        for there in corner_z + [opposite]:
            pl.semaphore_signal(barrier, inc=1, device_id=there, device_id_type=MESH)

    neighbours = 14 + has_top.astype(jnp.int32) + has_bottom.astype(jnp.int32) + 5 * at_corner.astype(jnp.int32)
    pl.semaphore_wait(barrier, neighbours)

    main = []
    for half in range(2):
        ch = pl.ds(half * 256, 256)
        for i, (frame, slot, there) in enumerate(((0, NEXT, down), (1, PREV, up))):
            main.append(
                pltpu.make_async_remote_copy(
                    x_hbm.at[frame, :, :, ch], raw.at[slot, pl.ds(1, 8), :, ch],
                    send_main.at[i, half], recv_main.at[i, half], device_id=there, device_id_type=MESH,
                )
            )

    def edge_copies(side, to_late):
        here, lower, upper = above(2 * side - 1)
        row, there_row = (0, 9) if side == 0 else (7, 0)
        copies = []
        targets = ((EVEN, 0, here), (ODD, 1, here), (NEXT, 0, lower), (PREV, 1, upper))
        for slot, frame, there in targets if to_late else targets[:2]:
            target = late_raw.at[slot] if to_late else raw.at[slot, there_row]
            copies.append(
                pltpu.make_async_remote_copy(
                    x_hbm.at[frame, row], target, send_edge.at[slot, side], recv_edge.at[slot, side],
                    device_id=there, device_id_type=MESH,
                )
            )
        return copies

    for c in main[:2]:
        c.start()

    @pl.when(has_top)
    def _():
        for c in edge_copies(0, False):
            c.start()

    @pl.when(has_bottom)
    def _():
        for c in edge_copies(1, False):
            c.start()

    for there in column + near_z:
        pl.semaphore_signal(know_plane, inc=1, device_id=there, device_id_type=MESH)

    @pl.when(at_corner)
    def _():
        for there in near_z + corner_z + [opposite]:
            pl.semaphore_signal(know_column, inc=1, device_id=there, device_id_type=MESH)

    small = [
        pltpu.make_async_copy(a, b, sem_small.at[1 + i])
        for i, (a, b) in enumerate(((bm_hbm, bm), (bl_hbm, bl)))
    ]
    for c in small:
        c.start()
    load_taps = pltpu.make_async_copy(wl_hbm, taps, sem_small.at[3])
    load_taps.start()

    shifted[:, 0:8] = jnp.zeros((10, 8, 256), f32)
    shifted[:, 40:48] = jnp.zeros((10, 8, 256), f32)
    late_raw_zero = jnp.zeros((32, 512), bf16)

    def silu(v):
        return v / (1.0 + jnp.exp(-v))

    def prepare(slot, half):
        ch = slice(half * 256, half * 256 + 256)
        v = silu(raw[slot, :, :, ch].astype(f32))
        act[slot, 1, :, :, ch] = v.astype(bf16)
        shifted[:, 8:40] = v
        act[slot, 0, :, :, ch] = shifted[:, 7:39].astype(bf16)
        act[slot, 2, :, :, ch] = shifted[:, 9:41].astype(bf16)

    def forwards(side):
        row = 9 if side == 0 else 0
        return [
            pltpu.make_async_remote_copy(
                raw.at[slot, row], raw.at[to, row], send_edge.at[to, side], recv_edge.at[to, side],
                device_id=there, device_id_type=MESH,
            )
            for slot, to, there in ((EVEN, NEXT, down), (ODD, PREV, up))
        ]

    def await_edges(slot, band):
        top, bottom = band % 32 != 0, band % 32 != 31
        for there, row, side in ((top, 0, 1), (bottom, 9, 0)):

            @pl.when(there)
            def _():
                pltpu.make_async_copy(late_raw.at[slot], raw.at[slot, row], recv_edge.at[slot, side]).wait()

            @pl.when(jnp.logical_not(there))
            def _():
                raw[slot, row] = late_raw_zero

    wl[...] = jnp.zeros_like(wl)
    load_taps.wait()
    for k in range(3):
        for i in range(3):
            for j in range(3):
                wl[j, k * 128 + i * 16 : k * 128 + i * 16 + 16] = taps[k, i, j]

    load_clips.wait()
    one, two = clips[0], clips[0] + clips[1]
    three = two + clips[2]

    def age(frame):
        begin = jnp.where(three <= frame, three, jnp.where(two <= frame, two, jnp.where(one <= frame, one, 0)))
        return frame - begin

    ages = [age((2 * s + 1 + d) % 16) for d in range(4)]
    lags = [[jnp.minimum(k, a) for k in range(3)] for a in ages]
    source = [[ODD - lags[0][k] for k in range(3)], [NEXT - lags[1][k] for k in range(3)]]
    source[0][0], source[1][0] = ODD, NEXT

    for first, second in ((main[0], main[2]), (main[1], main[3])):
        first.wait_send()
        second.start()
    pl.semaphore_wait(know_plane, 7)
    for there in near_z + corner_z:
        pl.semaphore_signal(know_four, inc=1, device_id=there, device_id_type=MESH)

    load_x.wait()
    await_edges(EVEN, h)
    await_edges(ODD, h)
    for side, there in ((0, has_bottom), (1, has_top)):

        @pl.when(there)
        def _():
            for c in forwards(side):
                c.start()

    for slot in (ODD, EVEN):
        for half in range(2):
            prepare(slot, half)

    acc[...] = jnp.zeros_like(acc)

    def await_weights(k):
        for n in range(3 * k, 3 * k + 3):
            load_w[n].wait()
            if n + 3 < 9:
                load_w[n + 3].start()

    def add_taps(output, k, half):
        slot = source[output][k]
        ch = slice(half * 256, half * 256 + 256)
        lhs = jnp.concatenate(
            [act[slot, j, i : i + 8, :, ch].reshape(256, 256) for i in range(3) for j in range(3)], axis=1
        )
        rhs = wm[k, :, :, ch].reshape(9 * 256, 512)
        acc[output] += jnp.dot(lhs, rhs, preferred_element_type=f32)

    await_weights(0)
    add_taps(0, 0, 0)
    add_taps(0, 0, 1)
    await_weights(1)
    add_taps(0, 1, 0)
    add_taps(0, 1, 1)
    pl.semaphore_wait(know_four, 8)
    for there in (corner_z[0], corner_z[3]):
        pl.semaphore_signal(know_all, inc=1, device_id=there, device_id_type=MESH)

    @pl.when(at_corner)
    def _():
        pl.semaphore_wait(know_column, 9)
        for there in (corner_z[0], corner_z[3]):
            pl.semaphore_signal(know_corners, inc=1, device_id=there, device_id_type=MESH)

    await_weights(2)
    await_edges(NEXT, band_next)
    await_edges(PREV, band_prev)
    for half in range(2):
        main[2 * half].wait_recv()
        main[2 * half + 1].wait_recv()
        prepare(NEXT, half)
        prepare(PREV, half)
        add_taps(0, 2, half)
        add_taps(1, 0, half)
        add_taps(1, 1, half)
        add_taps(1, 2, half)
        if half == 1:
            continue

        @pl.when(at_corner)
        def _():
            pl.semaphore_wait(know_corners, 2)

        for side, far in ((0, 32), (1, 31)):

            @pl.when(h == far)
            def _():
                for c in edge_copies(side, True):
                    c.start()

    pl.semaphore_wait(know_all, 2)

    def is_edge(band):
        return jnp.logical_or(band == 31, band == 32)

    late_slots = ((EVEN, is_edge(h)), (ODD, is_edge(h)), (NEXT, is_edge(band_next)), (PREV, is_edge(band_prev)))

    @pl.when(jnp.logical_or(is_edge(h), is_edge(other)))
    def _():
        at_bottom = h % 32 == 31
        for slot, is_late in late_slots:

            @pl.when(jnp.logical_and(is_late, at_bottom))
            def _():
                pltpu.make_async_copy(late_raw.at[slot], late_raw.at[slot], recv_edge.at[slot, 0]).wait()

            @pl.when(jnp.logical_and(is_late, jnp.logical_not(at_bottom)))
            def _():
                pltpu.make_async_copy(late_raw.at[slot], late_raw.at[slot], recv_edge.at[slot, 1]).wait()

            @pl.when(jnp.logical_not(is_late))
            def _():
                late_raw[slot] = late_raw_zero

        for half in range(2):
            ch = slice(half * 256, half * 256 + 256)
            v = silu(late_raw[:, :, ch].astype(f32))
            late[:, 1, :, ch] = v.astype(bf16)
            shifted[0:4, 8:40] = v
            late[:, 0, :, ch] = shifted[0:4, 7:39].astype(bf16)
            late[:, 2, :, ch] = shifted[0:4, 9:41].astype(bf16)
        row = jnp.where(at_bottom, 7, 0)
        tap = jnp.where(at_bottom, 2, 0)
        total = None
        for k in range(3):
            lhs = jnp.concatenate(
                [jnp.concatenate([late[source[o][k], j] for j in range(3)], axis=1) for o in range(2)], axis=0
            )
            part = jnp.dot(lhs, wm[k, tap].reshape(3 * 512, 512), preferred_element_type=f32)
            total = part if total is None else total + part
        acc[:, pl.ds(pl.multiple_of(row * 32, 32), 32)] += total.reshape(2, 32, 512)

    small[0].wait()
    for output, slot in ((0, ODD), (1, NEXT)):
        here = raw[slot, 1:9].reshape(256, 512).astype(f32)
        hidden = (here + acc[output] + bm[...]).astype(bf16).astype(f32)
        act2[output] = silu(hidden).astype(bf16)

    conv2[:, :, :, 0:8] = jnp.zeros((3, 3, 16, 8, 128), f32)
    conv2[:, :, :, 40:48] = jnp.zeros((3, 3, 16, 8, 128), f32)
    for j in range(3):
        product = lax.dot_general(
            act2[...].reshape(512, 512), wl[j], (((1,), (1,)), ((), ())), preferred_element_type=f32
        )
        for k in range(3):
            conv2[k, j, :, 8:40] = product[:, k * 128 : k * 128 + 128].reshape(16, 32, 128)
    lane = lax.broadcasted_iota(jnp.int32, (16, 128), 1)
    groups = [lane // 16 == n for n in range(8)]
    totals = [[[] for _ in range(3)] for _ in range(4)]
    for parity in range(2):
        for d in range(4):
            value = None
            for dest, output, lag, taps in ROUTES:
                if dest != d:
                    continue
                for k in taps:
                    keep = (lags[d][k] == lag).astype(f32)
                    summed = None
                    for j in range(3):
                        part = conv2[k, j, output * 8 : output * 8 + 8, pl.ds(7 + j + parity, 16, stride=2)]
                        summed = part if summed is None else summed + part
                    summed = summed * keep
                    value = summed if value is None else value + summed
            for r in range(8):
                for i in range(3):
                    place = r - i + 3
                    index, a = place // 2, place % 2
                    group = index // 3 * 4 + a * 2 + parity
                    turned = pltpu.roll(value[r], (group - i) * 16 % 128, 1)
                    totals[d][index % 3].append(jnp.where(groups[group], turned, 0.0))
    for d in range(4):
        for n in range(3):
            outgoing[d, n] = functools.reduce(lambda p, q: p + q, totals[d][n])

    for d in range(4):
        frame = (2 * s + 1 + d) % 16
        band = h if d == 0 else band_next
        role = d // 2
        slot = band % 32
        side = band // 32

        def send(q, there_core, target, sems, mine):
            there = (frame // 2, (frame % 2) * 32 + 2 * q + there_core)
            src = outgoing.at[d, :, q]
            if not mine:
                pltpu.make_async_remote_copy(
                    src, target, sems[0], sems[1], device_id=there, device_id_type=MESH
                ).start()
                return
            is_self = jnp.logical_and(there[0] == s, there[1] == h)

            @pl.when(is_self)
            def _():
                pltpu.make_async_copy(src, target, sems[1]).start()

            @pl.when(jnp.logical_not(is_self))
            def _():
                pltpu.make_async_remote_copy(
                    src, target, sems[0], sems[1], device_id=there, device_id_type=MESH
                ).start()

        @pl.loop(0, 16)
        def _(q):
            send(q, side, incoming.at[role, :, slot], (send_patch.at[d], recv_patch.at[role]), d == 0)

        @pl.when(is_edge(band))
        def _():
            @pl.loop(0, 16)
            def _(q):
                send(q, 1 - side, incoming.at[role, :, 32], (send_extra.at[d], recv_extra.at[role]), d == 0)

    small[1].wait()

    for role in range(2):
        arrived = incoming.at[role, :, pl.ds(0, 32)]
        pltpu.make_async_copy(arrived, arrived, recv_patch.at[role]).wait()
        arrived = incoming.at[role, :, 32]
        pltpu.make_async_copy(arrived, arrived, recv_extra.at[role]).wait()
    total = incoming[0] + incoming[1]
    band_row = lax.broadcasted_iota(jnp.int32, (32, 64), 0)
    piece = [total[n % 3, 0:32, (n // 3) * 64 : (n // 3) * 64 + 64] for n in range(6)]
    extra = total[:, 32:33]
    before = jnp.where(core == 1, extra[2, :, 64:128], 0.0)
    after = jnp.where(core == 0, extra[0, :, 0:64], 0.0)
    piece[1] += jnp.where(band_row == 0, before, pltpu.roll(piece[5], 1, 0))
    piece[4] += jnp.where(band_row == 31, after, pltpu.roll(piece[0], 31, 0))
    for n in range(4):
        patches[pl.ds(n, 32, stride=4), 0:64] = piece[1 + n]
    bias = jnp.concatenate([bl[...]] * 4, axis=1)
    latent = ((patches[:, 0:64] + bias) * latent_scale).astype(bf16)
    at = lax.broadcasted_iota(jnp.int32, (64, 64), 0)
    to = lax.broadcasted_iota(jnp.int32, (64, 64), 1)
    move = (to == (at % 16) * 4 + at // 16).astype(bf16)
    out[...] = jnp.dot(latent, move, preferred_element_type=f32).astype(bf16)
    write = pltpu.make_async_copy(out, out_hbm, sem_out)
    write.start()

    for c in main[2:]:
        c.wait_send()
    for side, there in ((0, has_bottom), (1, has_top)):

        @pl.when(there)
        def _():
            for c in forwards(side):
                c.wait_send()

    for side, sends in ((0, h != 0), (1, h != 63)):

        @pl.when(sends)
        def _():
            for c in edge_copies(side, False):
                c.wait_send()

    for side, far in ((0, 32), (1, 31)):

        @pl.when(h == far)
        def _():
            for c in edge_copies(side, True)[2:]:
                c.wait_send()

    for d in range(4):
        band = h if d == 0 else band_next
        if d == 0:
            own = jnp.logical_and(zh == 1, core == 1)
            own_extra = h == 32
        else:
            own = own_extra = None
        for sem, sent, one_less in ((send_patch.at[d], None, own), (send_extra.at[d], is_edge(band), own_extra)):
            whole, less = outgoing.at[d], outgoing.at[d, :, pl.ds(0, 15)]

            def finish(sem=sem, one_less=one_less, whole=whole, less=less):
                if one_less is None:
                    pltpu.make_async_copy(whole, whole, sem).wait()
                    return

                @pl.when(one_less)
                def _():
                    pltpu.make_async_copy(less, less, sem).wait()

                @pl.when(jnp.logical_not(one_less))
                def _():
                    pltpu.make_async_copy(whole, whole, sem).wait()

            if sent is None:
                finish()
            else:
                pl.when(sent)(finish)
    write.wait()


def per_device(features, clip_frames, conv_mid, bias_mid, conv_latent, bias_latent, patch_weight, patch_bias):
    dma, regular = pltpu.SemaphoreType.DMA, pltpu.SemaphoreType.REGULAR
    anywhere = pl.BlockSpec(memory_space=pl.ANY)
    latent_patches = pl.pallas_call(
        kernel,
        out_shape=jax.ShapeDtypeStruct((128, 64), bf16),
        in_specs=[anywhere] * 6,
        out_specs=anywhere,
        scratch_shapes=[
            pltpu.VMEM((4, 10, 32, 512), bf16),
            pltpu.VMEM((4, 3, 10, 32, 512), bf16),
            pltpu.VMEM((10, 48, 256), f32),
            pltpu.VMEM((3, 3, 3, 512, 512), bf16),
            pltpu.VMEM((2, 256, 512), f32),
            pltpu.VMEM((4, 32, 512), bf16),
            pltpu.VMEM((4, 3, 32, 512), bf16),
            pltpu.VMEM((2, 256, 512), bf16),
            pltpu.VMEM((3, 3, 3, 16, 512), bf16),
            pltpu.VMEM((3, 384, 512), bf16),
            pltpu.VMEM((3, 3, 16, 48, 128), f32),
            pltpu.VMEM((4, 3, 16, 128), f32),
            pltpu.VMEM((2, 3, 40, 128), f32),
            pltpu.VMEM((128, 128), f32),
            pltpu.VMEM((128, 64), bf16),
            pltpu.VMEM((1, 512), f32),
            pltpu.VMEM((1, 16), f32),
            pltpu.SMEM((4,), jnp.int32),
            dma, dma((9,)), dma((4,)), dma,
            dma((2, 2)), dma((2, 2)), dma((4, 2)), dma((4, 2)),
            dma((4,)), dma((2,)), dma((4,)), dma((2,)),
            regular, regular, regular, regular, regular,
        ],
        compiler_params=pltpu.CompilerParams(
            collective_id=0, has_side_effects=True, vmem_limit_bytes=58 * 2**20
        ),
    )(
        features, clip_frames, conv_mid, bias_mid.reshape(1, -1), jnp.swapaxes(conv_latent, 3, 4),
        bias_latent.reshape(1, -1),
    )
    product = jnp.dot(latent_patches, patch_weight, preferred_element_type=f32)
    return (product + patch_bias).astype(bf16)


def solution(mesh):
    return jax.shard_map(
        per_device,
        mesh=mesh,
        in_specs=(P("tm", "height", None, None), P(), P(), P(), P(), P(), P(), P()),
        out_specs=P(("tm", "height"), None),
        check_vma=False,
    )
```

```python
import functools

import jax
import jax.numpy as jnp
from jax import lax
from jax.experimental import pallas as pl
from jax.experimental.pallas import tpu as pltpu
from jax.sharding import PartitionSpec as P

latent_scale = 0.476986
MESH = pl.DeviceIdType.MESH
f32, bf16 = jnp.float32, jnp.bfloat16

PREV, EVEN, ODD, NEXT = range(4)
ROUTES = (
    (0, 0, 0, (0, 1, 2)),
    (1, 0, 1, (1, 2)),
    (1, 1, 0, (0, 1, 2)),
    (2, 0, 2, (2,)),
    (2, 1, 1, (1, 2)),
    (3, 1, 2, (2,)),
)


def device(s, zh, y, x, core):
    return (s, zh * 32 + y * 8 + x * 2 + core)


def kernel(
    x_hbm, clips_hbm, wm_hbm, bm_hbm, wl_hbm, bl_hbm, out_hbm,
    raw, act, shifted, wm, acc, late_raw, late, act2, taps, wl, conv2, outgoing, incoming, patches, out, bm, bl, clips,
    sem_x, sem_w, sem_small, sem_out, send_main, recv_main, send_edge, recv_edge, send_patch, recv_patch, send_extra, recv_extra,
    know_plane, know_four, know_all, know_column, know_corners,
):
    s, h = lax.axis_index("tm"), lax.axis_index("height")
    zh, y, x, core = h // 32, (h // 8) % 4, (h // 2) % 4, h % 2
    other = (h + 32) % 64
    z = zh * 8 + s

    def along_z(step):
        there = (z + step + 16) % 16
        return device(there % 8, there // 8, y, x, core)

    def above(step):
        band = (h + step + 64) % 64
        wrapped = (band + 32) % 64
        down = ((s + 7) % 8, jnp.where(s == 0, wrapped, band))
        up = ((s + 1) % 8, jnp.where(s == 7, wrapped, band))
        return (s, band), down, up

    has_top, has_bottom = h % 32 != 0, h % 32 != 31
    (_, down, up) = above(0)
    band_next = jnp.where(s == 7, other, h)
    band_prev = jnp.where(s == 0, other, h)

    load_x = pltpu.make_async_copy(x_hbm, raw.at[pl.ds(EVEN, 2), pl.ds(1, 8)], sem_x)
    load_x.start()
    load_w = [pltpu.make_async_copy(wm_hbm.at[k, i], wm.at[k, i], sem_w.at[3 * k + i]) for k in range(3) for i in range(3)]
    load_clips = pltpu.make_async_copy(clips_hbm, clips, sem_small.at[0])
    load_clips.start()
    for c in load_w[:3]:
        c.start()

    line = [device(s, zh, y, (x + d) % 4, c) for d in (1, 2, 3) for c in (0, 1)] + [device(s, zh, y, x, 1 - core)]
    column = [device(s, zh, (y + d) % 4, x, core) for d in (1, 2, 3)]
    near_z = [along_z(d) for d in (-2, -1, 1, 2)]
    barrier = pltpu.get_barrier_semaphore()
    for there in line + column + near_z:
        pl.semaphore_signal(barrier, inc=1, device_id=there, device_id_type=MESH)

    @pl.when(has_top)
    def _():
        pl.semaphore_signal(barrier, inc=1, device_id=above(-1)[0], device_id_type=MESH)

    @pl.when(has_bottom)
    def _():
        pl.semaphore_signal(barrier, inc=1, device_id=above(1)[0], device_id_type=MESH)

    at_corner = jnp.logical_or(h % 32 == 0, h % 32 == 31)
    opposite = (s, zh * 32 + 31 - h % 32)
    corner_z = [along_z(d) for d in (-4, -3, 3, 4)]

    @pl.when(at_corner)
    def _():
        for there in corner_z + [opposite]:
            pl.semaphore_signal(barrier, inc=1, device_id=there, device_id_type=MESH)

    neighbours = 14 + has_top.astype(jnp.int32) + has_bottom.astype(jnp.int32) + 5 * at_corner.astype(jnp.int32)
    pl.semaphore_wait(barrier, neighbours)

    main = []
    for half in range(2):
        ch = pl.ds(half * 256, 256)
        for i, (frame, slot, there) in enumerate(((0, NEXT, down), (1, PREV, up))):
            main.append(
                pltpu.make_async_remote_copy(
                    x_hbm.at[frame, :, :, ch], raw.at[slot, pl.ds(1, 8), :, ch],
                    send_main.at[i, half], recv_main.at[i, half], device_id=there, device_id_type=MESH,
                )
            )

    def edge_copies(side, to_late):
        here, lower, upper = above(2 * side - 1)
        row, there_row = (0, 9) if side == 0 else (7, 0)
        copies = []
        targets = ((EVEN, 0, here), (ODD, 1, here), (NEXT, 0, lower), (PREV, 1, upper))
        for slot, frame, there in targets if to_late else targets[:2]:
            target = late_raw.at[slot] if to_late else raw.at[slot, there_row]
            copies.append(
                pltpu.make_async_remote_copy(
                    x_hbm.at[frame, row], target, send_edge.at[slot, side], recv_edge.at[slot, side],
                    device_id=there, device_id_type=MESH,
                )
            )
        return copies

    for c in main[:2]:
        c.start()

    @pl.when(has_top)
    def _():
        for c in edge_copies(0, False):
            c.start()

    @pl.when(has_bottom)
    def _():
        for c in edge_copies(1, False):
            c.start()

    for there in column + near_z:
        pl.semaphore_signal(know_plane, inc=1, device_id=there, device_id_type=MESH)

    @pl.when(at_corner)
    def _():
        for there in near_z + corner_z + [opposite]:
            pl.semaphore_signal(know_column, inc=1, device_id=there, device_id_type=MESH)

    small = [
        pltpu.make_async_copy(a, b, sem_small.at[1 + i])
        for i, (a, b) in enumerate(((bm_hbm, bm), (bl_hbm, bl)))
    ]
    for c in small:
        c.start()
    load_taps = pltpu.make_async_copy(wl_hbm, taps, sem_small.at[3])
    load_taps.start()

    shifted[:, 0:8] = jnp.zeros((10, 8, 256), f32)
    shifted[:, 40:48] = jnp.zeros((10, 8, 256), f32)
    late_raw_zero = jnp.zeros((32, 512), bf16)

    def silu(v):
        return v / (1.0 + jnp.exp(-v))

    def prepare(slot, half, first, last):
        ch = slice(half * 256, half * 256 + 256)
        rows = slice(first, last)
        v = silu(raw[slot, rows, :, ch].astype(f32))
        act[slot, 1, rows, :, ch] = v.astype(bf16)
        shifted[rows, 8:40] = v
        act[slot, 0, rows, :, ch] = shifted[rows, 7:39].astype(bf16)
        act[slot, 2, rows, :, ch] = shifted[rows, 9:41].astype(bf16)

    def forwards(side):
        row = 9 if side == 0 else 0
        return [
            pltpu.make_async_remote_copy(
                raw.at[slot, row], raw.at[to, row], send_edge.at[to, side], recv_edge.at[to, side],
                device_id=there, device_id_type=MESH,
            )
            for slot, to, there in ((EVEN, NEXT, down), (ODD, PREV, up))
        ]

    def await_edges(slot, band):
        top, bottom = band % 32 != 0, band % 32 != 31
        for there, row, side in ((top, 0, 1), (bottom, 9, 0)):

            @pl.when(there)
            def _():
                pltpu.make_async_copy(late_raw.at[slot], raw.at[slot, row], recv_edge.at[slot, side]).wait()

            @pl.when(jnp.logical_not(there))
            def _():
                raw[slot, row] = late_raw_zero

    wl[...] = jnp.zeros_like(wl)
    load_taps.wait()
    for k in range(3):
        for i in range(3):
            for j in range(3):
                wl[j, k * 128 + i * 16 : k * 128 + i * 16 + 16] = taps[k, i, j]

    load_clips.wait()
    one, two = clips[0], clips[0] + clips[1]
    three = two + clips[2]

    def age(frame):
        begin = jnp.where(three <= frame, three, jnp.where(two <= frame, two, jnp.where(one <= frame, one, 0)))
        return frame - begin

    ages = [age((2 * s + 1 + d) % 16) for d in range(4)]
    lags = [[jnp.minimum(k, a) for k in range(3)] for a in ages]
    source = [[ODD - lags[0][k] for k in range(3)], [NEXT - lags[1][k] for k in range(3)]]
    source[0][0], source[1][0] = ODD, NEXT

    acc[...] = jnp.zeros_like(acc)

    def await_weights(k):
        for n in range(3 * k, 3 * k + 3):
            load_w[n].wait()
            if n + 3 < 9:
                load_w[n + 3].start()

    def add_rows(output, k, rows):
        slot = source[output][k]
        lhs = jnp.concatenate([act[slot, j, i : i + 8].reshape(256, 512) for i in rows for j in range(3)], axis=1)
        rhs = jnp.concatenate([wm[k, i].reshape(3 * 512, 512) for i in rows], axis=0)
        acc[output] += jnp.dot(lhs, rhs, preferred_element_type=f32)

    def add_taps(output, k, half):
        slot = source[output][k]
        ch = slice(half * 256, half * 256 + 256)
        lhs = jnp.concatenate(
            [act[slot, j, i : i + 8, :, ch].reshape(256, 256) for i in range(3) for j in range(3)], axis=1
        )
        rhs = wm[k, :, :, ch].reshape(9 * 256, 512)
        acc[output] += jnp.dot(lhs, rhs, preferred_element_type=f32)

    load_x.wait()
    for slot in (ODD, EVEN):
        for half in range(2):
            prepare(slot, half, 1, 9)
    await_weights(0)
    add_rows(0, 0, (1,))
    for c in main[2:]:
        c.start()
    await_weights(1)
    add_rows(0, 1, (1,))
    pl.semaphore_wait(know_plane, 7)
    for there in near_z + corner_z:
        pl.semaphore_signal(know_four, inc=1, device_id=there, device_id_type=MESH)

    @pl.when(at_corner)
    def _():
        pl.semaphore_wait(know_column, 9)
        for there in (corner_z[0], corner_z[3]):
            pl.semaphore_signal(know_corners, inc=1, device_id=there, device_id_type=MESH)

    await_edges(EVEN, h)
    await_edges(ODD, h)
    for side, there in ((0, has_bottom), (1, has_top)):

        @pl.when(there)
        def _():
            for c in forwards(side):
                c.start()

    for slot in (ODD, EVEN):
        for half in range(2):
            prepare(slot, half, 0, 1)
            prepare(slot, half, 9, 10)
    add_rows(0, 0, (0, 2))

    @pl.when(at_corner)
    def _():
        pl.semaphore_wait(know_corners, 2)

    for side, far in ((0, 32), (1, 31)):

        @pl.when(h == far)
        def _():
            for c in edge_copies(side, True):
                c.start()

    add_rows(0, 1, (0, 2))
    pl.semaphore_wait(know_four, 8)
    for there in (corner_z[0], corner_z[3]):
        pl.semaphore_signal(know_all, inc=1, device_id=there, device_id_type=MESH)

    await_weights(2)
    await_edges(NEXT, band_next)
    await_edges(PREV, band_prev)
    for half in range(2):
        main[2 * half].wait_recv()
        main[2 * half + 1].wait_recv()
        prepare(NEXT, half, 0, 10)
        prepare(PREV, half, 0, 10)
        add_taps(0, 2, half)
        add_taps(1, 0, half)
        add_taps(1, 1, half)
        add_taps(1, 2, half)
    pl.semaphore_wait(know_all, 2)

    def is_edge(band):
        return jnp.logical_or(band == 31, band == 32)

    late_slots = ((EVEN, is_edge(h)), (ODD, is_edge(h)), (NEXT, is_edge(band_next)), (PREV, is_edge(band_prev)))

    @pl.when(jnp.logical_or(is_edge(h), is_edge(other)))
    def _():
        at_bottom = h % 32 == 31
        for slot, is_late in late_slots:

            @pl.when(jnp.logical_and(is_late, at_bottom))
            def _():
                pltpu.make_async_copy(late_raw.at[slot], late_raw.at[slot], recv_edge.at[slot, 0]).wait()

            @pl.when(jnp.logical_and(is_late, jnp.logical_not(at_bottom)))
            def _():
                pltpu.make_async_copy(late_raw.at[slot], late_raw.at[slot], recv_edge.at[slot, 1]).wait()

            @pl.when(jnp.logical_not(is_late))
            def _():
                late_raw[slot] = late_raw_zero

        for half in range(2):
            ch = slice(half * 256, half * 256 + 256)
            v = silu(late_raw[:, :, ch].astype(f32))
            late[:, 1, :, ch] = v.astype(bf16)
            shifted[0:4, 8:40] = v
            late[:, 0, :, ch] = shifted[0:4, 7:39].astype(bf16)
            late[:, 2, :, ch] = shifted[0:4, 9:41].astype(bf16)
        row = jnp.where(at_bottom, 7, 0)
        tap = jnp.where(at_bottom, 2, 0)
        total = None
        for k in range(3):
            lhs = jnp.concatenate(
                [jnp.concatenate([late[source[o][k], j] for j in range(3)], axis=1) for o in range(2)], axis=0
            )
            part = jnp.dot(lhs, wm[k, tap].reshape(3 * 512, 512), preferred_element_type=f32)
            total = part if total is None else total + part
        acc[:, pl.ds(pl.multiple_of(row * 32, 32), 32)] += total.reshape(2, 32, 512)

    small[0].wait()
    for output, slot in ((0, ODD), (1, NEXT)):
        here = raw[slot, 1:9].reshape(256, 512).astype(f32)
        hidden = (here + acc[output] + bm[...]).astype(bf16).astype(f32)
        act2[output] = silu(hidden).astype(bf16)

    conv2[:, :, :, 0:8] = jnp.zeros((3, 3, 16, 8, 128), f32)
    conv2[:, :, :, 40:48] = jnp.zeros((3, 3, 16, 8, 128), f32)
    for j in range(3):
        product = lax.dot_general(
            act2[...].reshape(512, 512), wl[j], (((1,), (1,)), ((), ())), preferred_element_type=f32
        )
        for k in range(3):
            conv2[k, j, :, 8:40] = product[:, k * 128 : k * 128 + 128].reshape(16, 32, 128)
    lane = lax.broadcasted_iota(jnp.int32, (16, 128), 1)
    groups = [lane // 16 == n for n in range(8)]
    totals = [[[] for _ in range(3)] for _ in range(4)]
    for parity in range(2):
        for d in range(4):
            value = None
            for dest, output, lag, taps in ROUTES:
                if dest != d:
                    continue
                for k in taps:
                    keep = (lags[d][k] == lag).astype(f32)
                    summed = None
                    for j in range(3):
                        part = conv2[k, j, output * 8 : output * 8 + 8, pl.ds(7 + j + parity, 16, stride=2)]
                        summed = part if summed is None else summed + part
                    summed = summed * keep
                    value = summed if value is None else value + summed
            for r in range(8):
                for i in range(3):
                    place = r - i + 3
                    index, a = place // 2, place % 2
                    group = index // 3 * 4 + a * 2 + parity
                    turned = pltpu.roll(value[r], (group - i) * 16 % 128, 1)
                    totals[d][index % 3].append(jnp.where(groups[group], turned, 0.0))
    for d in range(4):
        for n in range(3):
            outgoing[d, n] = functools.reduce(lambda p, q: p + q, totals[d][n])

    for d in range(4):
        frame = (2 * s + 1 + d) % 16
        band = h if d == 0 else band_next
        role = d // 2
        slot = band % 32
        side = band // 32

        def send(q, there_core, target, sems, mine):
            there = (frame // 2, (frame % 2) * 32 + 2 * q + there_core)
            src = outgoing.at[d, :, q]
            if not mine:
                pltpu.make_async_remote_copy(
                    src, target, sems[0], sems[1], device_id=there, device_id_type=MESH
                ).start()
                return
            is_self = jnp.logical_and(there[0] == s, there[1] == h)

            @pl.when(is_self)
            def _():
                pltpu.make_async_copy(src, target, sems[1]).start()

            @pl.when(jnp.logical_not(is_self))
            def _():
                pltpu.make_async_remote_copy(
                    src, target, sems[0], sems[1], device_id=there, device_id_type=MESH
                ).start()

        @pl.loop(0, 16)
        def _(q):
            send(q, side, incoming.at[role, :, slot], (send_patch.at[d], recv_patch.at[role]), d == 0)

        @pl.when(is_edge(band))
        def _():
            @pl.loop(0, 16)
            def _(q):
                send(q, 1 - side, incoming.at[role, :, 32], (send_extra.at[d], recv_extra.at[role]), d == 0)

    small[1].wait()

    for role in range(2):
        arrived = incoming.at[role, :, pl.ds(0, 32)]
        pltpu.make_async_copy(arrived, arrived, recv_patch.at[role]).wait()
        arrived = incoming.at[role, :, 32]
        pltpu.make_async_copy(arrived, arrived, recv_extra.at[role]).wait()
    total = incoming[0] + incoming[1]
    band_row = lax.broadcasted_iota(jnp.int32, (32, 64), 0)
    piece = [total[n % 3, 0:32, (n // 3) * 64 : (n // 3) * 64 + 64] for n in range(6)]
    extra = total[:, 32:33]
    before = jnp.where(core == 1, extra[2, :, 64:128], 0.0)
    after = jnp.where(core == 0, extra[0, :, 0:64], 0.0)
    piece[1] += jnp.where(band_row == 0, before, pltpu.roll(piece[5], 1, 0))
    piece[4] += jnp.where(band_row == 31, after, pltpu.roll(piece[0], 31, 0))
    for n in range(4):
        patches[pl.ds(n, 32, stride=4), 0:64] = piece[1 + n]
    bias = jnp.concatenate([bl[...]] * 4, axis=1)
    latent = ((patches[:, 0:64] + bias) * latent_scale).astype(bf16)
    at = lax.broadcasted_iota(jnp.int32, (64, 64), 0)
    to = lax.broadcasted_iota(jnp.int32, (64, 64), 1)
    move = (to == (at % 16) * 4 + at // 16).astype(bf16)
    out[...] = jnp.dot(latent, move, preferred_element_type=f32).astype(bf16)
    write = pltpu.make_async_copy(out, out_hbm, sem_out)
    write.start()

    for c in main:
        c.wait_send()
    for side, there in ((0, has_bottom), (1, has_top)):

        @pl.when(there)
        def _():
            for c in forwards(side):
                c.wait_send()

    for side, sends in ((0, h != 0), (1, h != 63)):

        @pl.when(sends)
        def _():
            for c in edge_copies(side, False):
                c.wait_send()

    for side, far in ((0, 32), (1, 31)):

        @pl.when(h == far)
        def _():
            for c in edge_copies(side, True)[2:]:
                c.wait_send()

    for d in range(4):
        band = h if d == 0 else band_next
        if d == 0:
            own = jnp.logical_and(zh == 1, core == 1)
            own_extra = h == 32
        else:
            own = own_extra = None
        for sem, sent, one_less in ((send_patch.at[d], None, own), (send_extra.at[d], is_edge(band), own_extra)):
            whole, less = outgoing.at[d], outgoing.at[d, :, pl.ds(0, 15)]

            def finish(sem=sem, one_less=one_less, whole=whole, less=less):
                if one_less is None:
                    pltpu.make_async_copy(whole, whole, sem).wait()
                    return

                @pl.when(one_less)
                def _():
                    pltpu.make_async_copy(less, less, sem).wait()

                @pl.when(jnp.logical_not(one_less))
                def _():
                    pltpu.make_async_copy(whole, whole, sem).wait()

            if sent is None:
                finish()
            else:
                pl.when(sent)(finish)
    write.wait()


def per_device(features, clip_frames, conv_mid, bias_mid, conv_latent, bias_latent, patch_weight, patch_bias):
    dma, regular = pltpu.SemaphoreType.DMA, pltpu.SemaphoreType.REGULAR
    anywhere = pl.BlockSpec(memory_space=pl.ANY)
    latent_patches = pl.pallas_call(
        kernel,
        out_shape=jax.ShapeDtypeStruct((128, 64), bf16),
        in_specs=[anywhere] * 6,
        out_specs=anywhere,
        scratch_shapes=[
            pltpu.VMEM((4, 10, 32, 512), bf16),
            pltpu.VMEM((4, 3, 10, 32, 512), bf16),
            pltpu.VMEM((10, 48, 256), f32),
            pltpu.VMEM((3, 3, 3, 512, 512), bf16),
            pltpu.VMEM((2, 256, 512), f32),
            pltpu.VMEM((4, 32, 512), bf16),
            pltpu.VMEM((4, 3, 32, 512), bf16),
            pltpu.VMEM((2, 256, 512), bf16),
            pltpu.VMEM((3, 3, 3, 16, 512), bf16),
            pltpu.VMEM((3, 384, 512), bf16),
            pltpu.VMEM((3, 3, 16, 48, 128), f32),
            pltpu.VMEM((4, 3, 16, 128), f32),
            pltpu.VMEM((2, 3, 40, 128), f32),
            pltpu.VMEM((128, 128), f32),
            pltpu.VMEM((128, 64), bf16),
            pltpu.VMEM((1, 512), f32),
            pltpu.VMEM((1, 16), f32),
            pltpu.SMEM((4,), jnp.int32),
            dma, dma((9,)), dma((4,)), dma,
            dma((2, 2)), dma((2, 2)), dma((4, 2)), dma((4, 2)),
            dma((4,)), dma((2,)), dma((4,)), dma((2,)),
            regular, regular, regular, regular, regular,
        ],
        compiler_params=pltpu.CompilerParams(
            collective_id=0, has_side_effects=True, vmem_limit_bytes=58 * 2**20
        ),
    )(
        features, clip_frames, conv_mid, bias_mid.reshape(1, -1), jnp.swapaxes(conv_latent, 3, 4),
        bias_latent.reshape(1, -1),
    )
    product = jnp.dot(latent_patches, patch_weight, preferred_element_type=f32)
    return (product + patch_bias).astype(bf16)


def solution(mesh):
    return jax.shard_map(
        per_device,
        mesh=mesh,
        in_specs=(P("tm", "height", None, None), P(), P(), P(), P(), P(), P(), P()),
        out_specs=P(("tm", "height"), None),
        check_vma=False,
    )
```

```python
import functools

import jax
import jax.numpy as jnp
from jax import lax
from jax.experimental import pallas as pl
from jax.experimental.pallas import tpu as pltpu
from jax.sharding import PartitionSpec as P

latent_scale = 0.476986
MESH = pl.DeviceIdType.MESH
f32, bf16 = jnp.float32, jnp.bfloat16

PREV, EVEN, ODD, NEXT = range(4)
ROUTES = (
    (0, 0, 0, (0, 1, 2)),
    (1, 0, 1, (1, 2)),
    (1, 1, 0, (0, 1, 2)),
    (2, 0, 2, (2,)),
    (2, 1, 1, (1, 2)),
    (3, 1, 2, (2,)),
)


def device(s, zh, y, x, core):
    return (s, zh * 32 + y * 8 + x * 2 + core)


def kernel(
    x_hbm, clips_hbm, wm_hbm, bm_hbm, wl_hbm, bl_hbm, out_hbm,
    raw, act, shifted, wm, acc, late_raw, late, act2, taps, wl, conv2, outgoing, incoming, patches, out, bm, bl, clips,
    sem_x, sem_w, sem_small, sem_out, send_main, recv_main, send_edge, recv_edge, send_patch, recv_patch, send_extra, recv_extra,
    know_plane, know_four, know_all, know_column, know_corners,
):
    s, h = lax.axis_index("tm"), lax.axis_index("height")
    zh, y, x, core = h // 32, (h // 8) % 4, (h // 2) % 4, h % 2
    other = (h + 32) % 64
    z = zh * 8 + s

    def along_z(step):
        there = (z + step + 16) % 16
        return device(there % 8, there // 8, y, x, core)

    def above(step):
        band = (h + step + 64) % 64
        wrapped = (band + 32) % 64
        down = ((s + 7) % 8, jnp.where(s == 0, wrapped, band))
        up = ((s + 1) % 8, jnp.where(s == 7, wrapped, band))
        return (s, band), down, up

    has_top, has_bottom = h % 32 != 0, h % 32 != 31
    (_, down, up) = above(0)
    band_next = jnp.where(s == 7, other, h)
    band_prev = jnp.where(s == 0, other, h)

    load_x = pltpu.make_async_copy(x_hbm, raw.at[pl.ds(EVEN, 2), pl.ds(1, 8)], sem_x)
    load_x.start()
    load_w = [pltpu.make_async_copy(wm_hbm.at[k, i], wm.at[k, i], sem_w.at[3 * k + i]) for k in range(3) for i in range(3)]
    load_clips = pltpu.make_async_copy(clips_hbm, clips, sem_small.at[0])
    load_clips.start()
    for c in load_w[:5]:
        c.start()

    line = [device(s, zh, y, (x + d) % 4, c) for d in (1, 2, 3) for c in (0, 1)] + [device(s, zh, y, x, 1 - core)]
    column = [device(s, zh, (y + d) % 4, x, core) for d in (1, 2, 3)]
    near_z = [along_z(d) for d in (-2, -1, 1, 2)]
    barrier = pltpu.get_barrier_semaphore()
    for there in line + column + near_z:
        pl.semaphore_signal(barrier, inc=1, device_id=there, device_id_type=MESH)

    @pl.when(has_top)
    def _():
        pl.semaphore_signal(barrier, inc=1, device_id=above(-1)[0], device_id_type=MESH)

    @pl.when(has_bottom)
    def _():
        pl.semaphore_signal(barrier, inc=1, device_id=above(1)[0], device_id_type=MESH)

    at_corner = jnp.logical_or(h % 32 == 0, h % 32 == 31)
    opposite = (s, zh * 32 + 31 - h % 32)
    corner_z = [along_z(d) for d in (-4, -3, 3, 4)]

    @pl.when(at_corner)
    def _():
        for there in corner_z + [opposite]:
            pl.semaphore_signal(barrier, inc=1, device_id=there, device_id_type=MESH)

    neighbours = 14 + has_top.astype(jnp.int32) + has_bottom.astype(jnp.int32) + 5 * at_corner.astype(jnp.int32)
    pl.semaphore_wait(barrier, neighbours)

    main = []
    for half in range(2):
        ch = pl.ds(half * 256, 256)
        for i, (frame, slot, there) in enumerate(((0, NEXT, down), (1, PREV, up))):
            main.append(
                pltpu.make_async_remote_copy(
                    x_hbm.at[frame, :, :, ch], raw.at[slot, pl.ds(1, 8), :, ch],
                    send_main.at[i, half], recv_main.at[i, half], device_id=there, device_id_type=MESH,
                )
            )

    def edge_copies(side, to_late):
        here, lower, upper = above(2 * side - 1)
        row, there_row = (0, 9) if side == 0 else (7, 0)
        copies = []
        targets = ((EVEN, 0, here), (ODD, 1, here), (NEXT, 0, lower), (PREV, 1, upper))
        for slot, frame, there in targets if to_late else targets[:2]:
            target = late_raw.at[slot] if to_late else raw.at[slot, there_row]
            copies.append(
                pltpu.make_async_remote_copy(
                    x_hbm.at[frame, row], target, send_edge.at[slot, side], recv_edge.at[slot, side],
                    device_id=there, device_id_type=MESH,
                )
            )
        return copies

    for c in main[:2]:
        c.start()

    @pl.when(has_top)
    def _():
        for c in edge_copies(0, False):
            c.start()

    @pl.when(has_bottom)
    def _():
        for c in edge_copies(1, False):
            c.start()

    for there in column + near_z:
        pl.semaphore_signal(know_plane, inc=1, device_id=there, device_id_type=MESH)

    @pl.when(at_corner)
    def _():
        for there in near_z + corner_z + [opposite]:
            pl.semaphore_signal(know_column, inc=1, device_id=there, device_id_type=MESH)

    small = [
        pltpu.make_async_copy(a, b, sem_small.at[1 + i])
        for i, (a, b) in enumerate(((bm_hbm, bm), (bl_hbm, bl)))
    ]
    for c in small:
        c.start()
    load_taps = pltpu.make_async_copy(wl_hbm, taps, sem_small.at[3])
    load_taps.start()

    shifted[:, 0:8] = jnp.zeros((10, 8, 256), f32)
    shifted[:, 40:48] = jnp.zeros((10, 8, 256), f32)
    late_raw_zero = jnp.zeros((32, 512), bf16)

    def silu(v):
        return v / (1.0 + jnp.exp(-v))

    def prepare(slot, half, first, last):
        ch = slice(half * 256, half * 256 + 256)
        rows = slice(first, last)
        v = silu(raw[slot, rows, :, ch].astype(f32))
        act[slot, 1, rows, :, ch] = v.astype(bf16)
        shifted[rows, 8:40] = v
        act[slot, 0, rows, :, ch] = shifted[rows, 7:39].astype(bf16)
        act[slot, 2, rows, :, ch] = shifted[rows, 9:41].astype(bf16)

    def forwards(side):
        row = 9 if side == 0 else 0
        return [
            pltpu.make_async_remote_copy(
                raw.at[slot, row], raw.at[to, row], send_edge.at[to, side], recv_edge.at[to, side],
                device_id=there, device_id_type=MESH,
            )
            for slot, to, there in ((EVEN, NEXT, down), (ODD, PREV, up))
        ]

    def await_edges(slot, band):
        top, bottom = band % 32 != 0, band % 32 != 31
        for there, row, side in ((top, 0, 1), (bottom, 9, 0)):

            @pl.when(there)
            def _():
                pltpu.make_async_copy(late_raw.at[slot], raw.at[slot, row], recv_edge.at[slot, side]).wait()

            @pl.when(jnp.logical_not(there))
            def _():
                raw[slot, row] = late_raw_zero

    wl[...] = jnp.zeros_like(wl)
    load_taps.wait()
    for k in range(3):
        for i in range(3):
            for j in range(3):
                wl[j, k * 128 + i * 16 : k * 128 + i * 16 + 16] = taps[k, i, j]

    load_clips.wait()
    one, two = clips[0], clips[0] + clips[1]
    three = two + clips[2]

    def age(frame):
        begin = jnp.where(three <= frame, three, jnp.where(two <= frame, two, jnp.where(one <= frame, one, 0)))
        return frame - begin

    ages = [age((2 * s + 1 + d) % 16) for d in range(4)]
    lags = [[jnp.minimum(k, a) for k in range(3)] for a in ages]
    source = [[ODD - lags[0][k] for k in range(3)], [NEXT - lags[1][k] for k in range(3)]]
    source[0][0], source[1][0] = ODD, NEXT

    acc[...] = jnp.zeros_like(acc)

    def await_weights(k):
        for n in range(3 * k, 3 * k + 3):
            load_w[n].wait()
            if n + 5 < 9:
                load_w[n + 5].start()

    def add_rows(output, k, rows):
        slot = source[output][k]
        lhs = jnp.concatenate([act[slot, j, i : i + 8].reshape(256, 512) for i in rows for j in range(3)], axis=1)
        rhs = jnp.concatenate([wm[k, i].reshape(3 * 512, 512) for i in rows], axis=0)
        acc[output] += jnp.dot(lhs, rhs, preferred_element_type=f32)

    def add_taps(output, k, half):
        slot = source[output][k]
        ch = slice(half * 256, half * 256 + 256)
        lhs = jnp.concatenate(
            [act[slot, j, i : i + 8, :, ch].reshape(256, 256) for i in range(3) for j in range(3)], axis=1
        )
        rhs = wm[k, :, :, ch].reshape(9 * 256, 512)
        acc[output] += jnp.dot(lhs, rhs, preferred_element_type=f32)

    load_x.wait()
    for slot in (ODD, EVEN):
        for half in range(2):
            prepare(slot, half, 1, 9)
    await_weights(0)
    add_rows(0, 0, (1,))
    for c in main[2:]:
        c.start()
    await_weights(1)
    add_rows(0, 1, (1,))
    pl.semaphore_wait(know_plane, 7)
    for there in near_z + corner_z:
        pl.semaphore_signal(know_four, inc=1, device_id=there, device_id_type=MESH)

    @pl.when(at_corner)
    def _():
        pl.semaphore_wait(know_column, 9)
        for there in (corner_z[0], corner_z[3]):
            pl.semaphore_signal(know_corners, inc=1, device_id=there, device_id_type=MESH)

    await_edges(EVEN, h)
    await_edges(ODD, h)
    for side, there in ((0, has_bottom), (1, has_top)):

        @pl.when(there)
        def _():
            for c in forwards(side):
                c.start()

    for slot in (ODD, EVEN):
        for half in range(2):
            prepare(slot, half, 0, 1)
            prepare(slot, half, 9, 10)
    add_rows(0, 0, (0, 2))

    @pl.when(at_corner)
    def _():
        pl.semaphore_wait(know_corners, 2)

    for side, far in ((0, 32), (1, 31)):

        @pl.when(h == far)
        def _():
            for c in edge_copies(side, True):
                c.start()

    add_rows(0, 1, (0, 2))
    pl.semaphore_wait(know_four, 8)
    for there in (corner_z[0], corner_z[3]):
        pl.semaphore_signal(know_all, inc=1, device_id=there, device_id_type=MESH)

    await_weights(2)
    await_edges(NEXT, band_next)
    await_edges(PREV, band_prev)
    for half in range(2):
        main[2 * half].wait_recv()
        main[2 * half + 1].wait_recv()
        prepare(NEXT, half, 0, 10)
        prepare(PREV, half, 0, 10)
        add_taps(0, 2, half)
        add_taps(1, 0, half)
        add_taps(1, 1, half)
        add_taps(1, 2, half)
    pl.semaphore_wait(know_all, 2)

    def is_edge(band):
        return jnp.logical_or(band == 31, band == 32)

    late_slots = ((EVEN, is_edge(h)), (ODD, is_edge(h)), (NEXT, is_edge(band_next)), (PREV, is_edge(band_prev)))

    @pl.when(jnp.logical_or(is_edge(h), is_edge(other)))
    def _():
        at_bottom = h % 32 == 31
        for slot, is_late in late_slots:

            @pl.when(jnp.logical_and(is_late, at_bottom))
            def _():
                pltpu.make_async_copy(late_raw.at[slot], late_raw.at[slot], recv_edge.at[slot, 0]).wait()

            @pl.when(jnp.logical_and(is_late, jnp.logical_not(at_bottom)))
            def _():
                pltpu.make_async_copy(late_raw.at[slot], late_raw.at[slot], recv_edge.at[slot, 1]).wait()

            @pl.when(jnp.logical_not(is_late))
            def _():
                late_raw[slot] = late_raw_zero

        for half in range(2):
            ch = slice(half * 256, half * 256 + 256)
            v = silu(late_raw[:, :, ch].astype(f32))
            late[:, 1, :, ch] = v.astype(bf16)
            shifted[0:4, 8:40] = v
            late[:, 0, :, ch] = shifted[0:4, 7:39].astype(bf16)
            late[:, 2, :, ch] = shifted[0:4, 9:41].astype(bf16)
        row = jnp.where(at_bottom, 7, 0)
        tap = jnp.where(at_bottom, 2, 0)
        total = None
        for k in range(3):
            lhs = jnp.concatenate(
                [jnp.concatenate([late[source[o][k], j] for j in range(3)], axis=1) for o in range(2)], axis=0
            )
            part = jnp.dot(lhs, wm[k, tap].reshape(3 * 512, 512), preferred_element_type=f32)
            total = part if total is None else total + part
        acc[:, pl.ds(pl.multiple_of(row * 32, 32), 32)] += total.reshape(2, 32, 512)

    small[0].wait()
    for output, slot in ((0, ODD), (1, NEXT)):
        here = raw[slot, 1:9].reshape(256, 512).astype(f32)
        hidden = (here + acc[output] + bm[...]).astype(bf16).astype(f32)
        act2[output] = silu(hidden).astype(bf16)

    conv2[:, :, :, 0:8] = jnp.zeros((3, 3, 16, 8, 128), f32)
    conv2[:, :, :, 40:48] = jnp.zeros((3, 3, 16, 8, 128), f32)
    for j in range(3):
        product = lax.dot_general(
            act2[...].reshape(512, 512), wl[j], (((1,), (1,)), ((), ())), preferred_element_type=f32
        )
        for k in range(3):
            conv2[k, j, :, 8:40] = product[:, k * 128 : k * 128 + 128].reshape(16, 32, 128)
    lane = lax.broadcasted_iota(jnp.int32, (16, 128), 1)
    groups = [lane // 16 == n for n in range(8)]
    totals = [[[] for _ in range(3)] for _ in range(4)]
    for parity in range(2):
        for d in range(4):
            value = None
            for dest, output, lag, taps in ROUTES:
                if dest != d:
                    continue
                for k in taps:
                    keep = (lags[d][k] == lag).astype(f32)
                    summed = None
                    for j in range(3):
                        part = conv2[k, j, output * 8 : output * 8 + 8, pl.ds(7 + j + parity, 16, stride=2)]
                        summed = part if summed is None else summed + part
                    summed = summed * keep
                    value = summed if value is None else value + summed
            for r in range(8):
                for i in range(3):
                    place = r - i + 3
                    index, a = place // 2, place % 2
                    group = index // 3 * 4 + a * 2 + parity
                    turned = pltpu.roll(value[r], (group - i) * 16 % 128, 1)
                    totals[d][index % 3].append(jnp.where(groups[group], turned, 0.0))
    for d in range(4):
        for n in range(3):
            outgoing[d, n] = functools.reduce(lambda p, q: p + q, totals[d][n])

    for d in range(4):
        frame = (2 * s + 1 + d) % 16
        band = h if d == 0 else band_next
        role = d // 2
        slot = band % 32
        side = band // 32

        def send(q, there_core, target, sems, mine):
            there = (frame // 2, (frame % 2) * 32 + 2 * q + there_core)
            src = outgoing.at[d, :, q]
            if not mine:
                pltpu.make_async_remote_copy(
                    src, target, sems[0], sems[1], device_id=there, device_id_type=MESH
                ).start()
                return
            is_self = jnp.logical_and(there[0] == s, there[1] == h)

            @pl.when(is_self)
            def _():
                pltpu.make_async_copy(src, target, sems[1]).start()

            @pl.when(jnp.logical_not(is_self))
            def _():
                pltpu.make_async_remote_copy(
                    src, target, sems[0], sems[1], device_id=there, device_id_type=MESH
                ).start()

        @pl.loop(0, 16)
        def _(q):
            send(q, side, incoming.at[role, :, slot], (send_patch.at[d], recv_patch.at[role]), d == 0)

        @pl.when(is_edge(band))
        def _():
            @pl.loop(0, 16)
            def _(q):
                send(q, 1 - side, incoming.at[role, :, 32], (send_extra.at[d], recv_extra.at[role]), d == 0)

    small[1].wait()

    for role in range(2):
        arrived = incoming.at[role, :, pl.ds(0, 32)]
        pltpu.make_async_copy(arrived, arrived, recv_patch.at[role]).wait()
        arrived = incoming.at[role, :, 32]
        pltpu.make_async_copy(arrived, arrived, recv_extra.at[role]).wait()
    total = incoming[0] + incoming[1]
    band_row = lax.broadcasted_iota(jnp.int32, (32, 64), 0)
    piece = [total[n % 3, 0:32, (n // 3) * 64 : (n // 3) * 64 + 64] for n in range(6)]
    extra = total[:, 32:33]
    before = jnp.where(core == 1, extra[2, :, 64:128], 0.0)
    after = jnp.where(core == 0, extra[0, :, 0:64], 0.0)
    piece[1] += jnp.where(band_row == 0, before, pltpu.roll(piece[5], 1, 0))
    piece[4] += jnp.where(band_row == 31, after, pltpu.roll(piece[0], 31, 0))
    for n in range(4):
        patches[pl.ds(n, 32, stride=4), 0:64] = piece[1 + n]
    bias = jnp.concatenate([bl[...]] * 4, axis=1)
    latent = ((patches[:, 0:64] + bias) * latent_scale).astype(bf16)
    at = lax.broadcasted_iota(jnp.int32, (64, 64), 0)
    to = lax.broadcasted_iota(jnp.int32, (64, 64), 1)
    move = (to == (at % 16) * 4 + at // 16).astype(bf16)
    out[...] = jnp.dot(latent, move, preferred_element_type=f32).astype(bf16)
    write = pltpu.make_async_copy(out, out_hbm, sem_out)
    write.start()

    for c in main:
        c.wait_send()
    for side, there in ((0, has_bottom), (1, has_top)):

        @pl.when(there)
        def _():
            for c in forwards(side):
                c.wait_send()

    for side, sends in ((0, h != 0), (1, h != 63)):

        @pl.when(sends)
        def _():
            for c in edge_copies(side, False):
                c.wait_send()

    for side, far in ((0, 32), (1, 31)):

        @pl.when(h == far)
        def _():
            for c in edge_copies(side, True)[2:]:
                c.wait_send()

    for d in range(4):
        band = h if d == 0 else band_next
        if d == 0:
            own = jnp.logical_and(zh == 1, core == 1)
            own_extra = h == 32
        else:
            own = own_extra = None
        for sem, sent, one_less in ((send_patch.at[d], None, own), (send_extra.at[d], is_edge(band), own_extra)):
            whole, less = outgoing.at[d], outgoing.at[d, :, pl.ds(0, 15)]

            def finish(sem=sem, one_less=one_less, whole=whole, less=less):
                if one_less is None:
                    pltpu.make_async_copy(whole, whole, sem).wait()
                    return

                @pl.when(one_less)
                def _():
                    pltpu.make_async_copy(less, less, sem).wait()

                @pl.when(jnp.logical_not(one_less))
                def _():
                    pltpu.make_async_copy(whole, whole, sem).wait()

            if sent is None:
                finish()
            else:
                pl.when(sent)(finish)
    write.wait()


def per_device(features, clip_frames, conv_mid, bias_mid, conv_latent, bias_latent, patch_weight, patch_bias):
    dma, regular = pltpu.SemaphoreType.DMA, pltpu.SemaphoreType.REGULAR
    anywhere = pl.BlockSpec(memory_space=pl.ANY)
    latent_patches = pl.pallas_call(
        kernel,
        out_shape=jax.ShapeDtypeStruct((128, 64), bf16),
        in_specs=[anywhere] * 6,
        out_specs=anywhere,
        scratch_shapes=[
            pltpu.VMEM((4, 10, 32, 512), bf16),
            pltpu.VMEM((4, 3, 10, 32, 512), bf16),
            pltpu.VMEM((10, 48, 256), f32),
            pltpu.VMEM((3, 3, 3, 512, 512), bf16),
            pltpu.VMEM((2, 256, 512), f32),
            pltpu.VMEM((4, 32, 512), bf16),
            pltpu.VMEM((4, 3, 32, 512), bf16),
            pltpu.VMEM((2, 256, 512), bf16),
            pltpu.VMEM((3, 3, 3, 16, 512), bf16),
            pltpu.VMEM((3, 384, 512), bf16),
            pltpu.VMEM((3, 3, 16, 48, 128), f32),
            pltpu.VMEM((4, 3, 16, 128), f32),
            pltpu.VMEM((2, 3, 40, 128), f32),
            pltpu.VMEM((128, 128), f32),
            pltpu.VMEM((128, 64), bf16),
            pltpu.VMEM((1, 512), f32),
            pltpu.VMEM((1, 16), f32),
            pltpu.SMEM((4,), jnp.int32),
            dma, dma((9,)), dma((4,)), dma,
            dma((2, 2)), dma((2, 2)), dma((4, 2)), dma((4, 2)),
            dma((4,)), dma((2,)), dma((4,)), dma((2,)),
            regular, regular, regular, regular, regular,
        ],
        compiler_params=pltpu.CompilerParams(
            collective_id=0, has_side_effects=True, vmem_limit_bytes=58 * 2**20
        ),
    )(
        features, clip_frames, conv_mid, bias_mid.reshape(1, -1), jnp.swapaxes(conv_latent, 3, 4),
        bias_latent.reshape(1, -1),
    )
    product = jnp.dot(latent_patches, patch_weight, preferred_element_type=f32)
    return (product + patch_bias).astype(bf16)


def solution(mesh):
    return jax.shard_map(
        per_device,
        mesh=mesh,
        in_specs=(P("tm", "height", None, None), P(), P(), P(), P(), P(), P(), P()),
        out_specs=P(("tm", "height"), None),
        check_vma=False,
    )
```
